256 devices in a mesh: prompt: 2 (over y_lo), tm: 16 (over x, y_hi, core), head: 8 (over z).
Axes of the slice: x: 4, y: 4 (y_hi: 2, y_lo: 2; y = y_hi * 2 + y_lo), z: 8, core: 2. Of those that a mesh axis runs over, the one named last changes fastest.
Arguments:
- queries: bfloat16 [49152, 3072], P(('prompt', 'tm'), 'head'), parts along dimension 0, may hold values from -11 to 11
- key_rows: bfloat16 [49152, 3072], P(('prompt', 'tm'), 'head'), parts along dimension 0, may hold values from -11 to 11
- values: bfloat16 [49152, 3072], P(('prompt', 'tm'), 'head'), parts along dimension 0, may hold values from -24 to 24
- out_weight: bfloat16 [3072, 3072], P('head'), may hold values from -0.109375 to 0.109375
- gate_scale: float32 [6144], P('prompt'), parts along dimension 0, may hold values from 0.5 to 2
- window: int32 [256, 8, 3], P(('prompt', 'tm')), parts along dimension 0, may hold values from -1 to 1, as said below
Outputs:
- layer_out: float32 [49152, 3072], P(('prompt', 'tm', 'head')), parts along dimension 0
The draws below stay inside these ranges and needn't reach their ends.
There are 2 independent parts, one for each index of `prompt`. The reference program is written for one: setup_inputs(seed, part) draws one part's arguments, and reference() takes and returns one part's arrays. A program takes and returns all parts, laid end to end along the dimension named above; an argument that names none is the same for every part. Nothing has to cross between parts.
Inputs may be any that keep to these rules, and one draw needn't show every extreme that they name: `window`: for each query tile the 8 offsets are distinct triples of -1, 0 and 1; the first is (0, 0, 0), the second has time offset 1 and the third time offset -1.
All inputs are finite; a program needn't handle non-finite values.
Results may differ from the reference program's by a relative error of at most 0.019.
Values may be sent and summed in bfloat16 or wider, within the bound.
A program may use at most 64 MiB of HBM per device.

```python
import math
import jax
import jax.numpy as jnp
from jax import lax

D = 3072
HEADS = 24
HD = 128
TILE_T = 3
TILE_H = 8
TILE_W = 8
NTH = 2
NTW = 4
KW = 8
TOK_DEV = 1536
TOKENS = 24576
TILES = 128
N_TM = 16
N_HEAD = 8


def query_key_pair(key):
    base = jax.random.fold_in(key, 11)
    first, second = jax.random.split(base, 2)
    shape = (TOKENS, D)
    q_draw = jnp.clip(1.2 * jax.random.normal(first, shape, jnp.float32), -7.0, 7.0)
    k_draw = jnp.clip(1.2 * jax.random.normal(second, shape, jnp.float32), -7.0, 7.0)
    return (q_draw, k_draw)


def draw_queries(key, part):
    return query_key_pair(key)[0].astype(jnp.bfloat16)


def draw_key_rows(key, part):
    return query_key_pair(key)[1].astype(jnp.bfloat16)


def draw_window(key, part):

    def one_tile(tile_key):
        first, second, third = jax.random.split(tile_key, 3)
        later = (18 + jax.random.randint(first, (), 0, 9)).astype(jnp.int32)
        earlier = jax.random.randint(second, (), 0, 9).astype(jnp.int32)
        order = jax.random.permutation(third, 27).astype(jnp.int32)
        excluded = (order == 13) | (order == later) | (order == earlier)
        ranked = order[jnp.argsort(excluded.astype(jnp.int32), stable=True)]
        remaining = ranked[:KW - 3]
        codes = jnp.concatenate([jnp.array([13], dtype=jnp.int32), later[None], earlier[None], remaining]).astype(jnp.int32)
        return jnp.stack([codes // 9 - 1, codes // 3 % 3 - 1, codes % 3 - 1], axis=-1).astype(jnp.int32)
    return jax.vmap(one_tile)(jax.random.split(jax.random.fold_in(key, 5), TILES))


def block_levels(stream_key, extent, shards, least, largest):
    level = 1.0
    for position, blocks in shards:
        draws = jax.random.uniform(jax.random.fold_in(jax.random.fold_in(stream_key, 6), position), (blocks,), jnp.float32, least / len(shards), largest / len(shards))
        level = level * jnp.repeat(jnp.exp(draws), extent[position] // blocks).reshape((-1,) + (1,) * (len(extent) - 1 - position))
    return level


def normal_values(rng, shape, width, limit, shards=(), held_as=jnp.bfloat16):
    result = jax.random.normal(rng, shape, jnp.float32) * width
    if len(shards) > 0:
        result = block_levels(rng, shape, shards, -0.22, 0.18) * result
    return jnp.clip(result, min=-limit, max=limit).astype(held_as)


def setup_inputs(seed: int = 0, part: int = 0) -> dict:
    streams_of = jax.random.split(jax.random.key(seed), 7)
    part_splits = jax.random.split(jax.random.fold_in(streams_of[6], part), 7)
    return {
        "queries": draw_queries(jax.random.fold_in(jax.random.fold_in(streams_of[6], part), 71), part),
        "key_rows": draw_key_rows(jax.random.fold_in(jax.random.fold_in(streams_of[6], part), 71), part),
        "values": normal_values(part_splits[2], (TOKENS, D), 4.0, 24.0, ((0, 16), (1, 8))),
        "out_weight": normal_values(streams_of[3], (D, D), D ** -0.5, 0.109375, ((0, 8),)),
        "gate_scale": jnp.clip(jax.random.uniform(part_splits[4], (D,), jnp.float32, 0.5, 2.0), 0.5, 2.0),
        "window": draw_window(jax.random.fold_in(jax.random.fold_in(streams_of[6], part), 71), part),
    }


neg_large = -1e+30

def tile_coords(tile_ids):
    return (tile_ids // (NTH * NTW), tile_ids // NTW % NTH, tile_ids % NTW)

def reference(queries, key_rows, values, out_weight, gate_scale, window):
    tile_tokens = TILE_T * TILE_H * TILE_W
    offsets = (window[..., 0] + 1) * 9 + (window[..., 1] + 1) * 3 + (window[..., 2] + 1)
    choices27 = jnp.arange(27, dtype=jnp.int32)
    allowed = jnp.any(offsets[:, :, None] == choices27[None, None, :], axis=1)
    tile_ids = jnp.arange(TILES, dtype=jnp.int32)
    t_pos, h_pos, w_pos = tile_coords(tile_ids)
    delta_time = t_pos[None, :] - t_pos[:, None]
    delta_height = h_pos[None, :] - h_pos[:, None]
    delta_width = w_pos[None, :] - w_pos[:, None]
    inside = (jnp.abs(delta_time) <= 1) & (jnp.abs(delta_height) <= 1) & (jnp.abs(delta_width) <= 1)
    codes = jnp.where(inside, (delta_time + 1) * 9 + (delta_height + 1) * 3 + (delta_width + 1), 0).astype(jnp.int32)
    tile_mask = inside & jnp.take_along_axis(allowed, codes, axis=1)
    token_tiles = jnp.arange(TOKENS, dtype=jnp.int32) // tile_tokens
    scaling = 1.0 / math.sqrt(HD)

    def one_head(head):
        q_head = lax.dynamic_slice_in_dim(queries, head * HD, HD, 1)
        k_head = lax.dynamic_slice_in_dim(key_rows, head * HD, HD, 1)
        v_head = lax.dynamic_slice_in_dim(values, head * HD, HD, 1)

        def one_block(index):
            q_block = lax.dynamic_slice_in_dim(q_head, index * TOK_DEV, TOK_DEV, 0)
            block_tiles = lax.dynamic_slice_in_dim(token_tiles, index * TOK_DEV, TOK_DEV, 0)
            permit = tile_mask[block_tiles][:, token_tiles]
            scores = jnp.dot(q_block, k_head.T, preferred_element_type=jnp.float32) * scaling
            top = lax.optimization_barrier(jnp.max(jnp.where(permit, scores, neg_large), axis=1, keepdims=True))
            weights = jnp.where(permit, jnp.exp(scores - top), 0.0)
            total = lax.optimization_barrier(jnp.sum(weights, axis=1, keepdims=True))
            numer = jnp.dot(weights.astype(jnp.bfloat16), v_head, preferred_element_type=jnp.float32)
            return numer / total
        return lax.map(one_block, jnp.arange(N_TM, dtype=jnp.int32)).reshape(TOKENS, HD)
    heads_out = lax.map(one_head, jnp.arange(HEADS, dtype=jnp.int32))
    attended = jnp.transpose(heads_out, (1, 0, 2)).reshape(TOKENS, HEADS * HD).astype(jnp.bfloat16)
    group_width = HEADS * HD // N_HEAD

    def add_group(group, summed):
        part_att = lax.dynamic_slice_in_dim(attended, group * group_width, group_width, 1)
        part_weight = lax.dynamic_slice_in_dim(out_weight, group * group_width, group_width, 0)
        term = jnp.dot(part_att, part_weight, preferred_element_type=jnp.float32).astype(jnp.bfloat16)
        term = lax.optimization_barrier(term)
        return summed + term.astype(jnp.float32)
    projected = lax.fori_loop(0, N_HEAD, add_group, jnp.zeros((TOKENS, D), jnp.float32))
    return gate_scale[None, :] * projected
```

```python
import functools
import math

import jax
import jax.numpy as jnp
from jax import lax
from jax.experimental import pallas as pl
from jax.experimental.pallas import tpu as pltpu
from jax.sharding import PartitionSpec as P

HD = 128
TILE = 192
NTH = 2
NTW = 4
SLOTS = 8
STAGGER = 4
MESH = pl.DeviceIdType.MESH
NEG = -1e30


def kernel(n_tm, n_head, n_local, q_hbm, k_hbm, v_hbm, w_hbm, window, out_hbm,
           qbuf, att, arecv, wbuf, acc, *rest):
    kbufs, vbufs = rest[:n_local], rest[n_local:2 * n_local]
    (loc_sem, out_sem, halo_send, halo_recv, core_send, core_recv, a_send, a_recv,
     ring_send, ring_recv, mate_send, mate_recv, pair_send, pair_recv) = rest[2 * n_local:]
    tokens = q_hbm.shape[0]
    tiles = tokens // TILE
    width = w_hbm.shape[1]
    half, quarter = width // 2, width // 4

    tm = lax.axis_index("tm")
    z = lax.axis_index("head")
    core = tm % 2
    x = tm // 4
    n_x = n_tm // 4
    parity = x % 2
    partner = {"tm": tm + 1 - 2 * core}
    far = {"tm": (tm - 1 + 2 * core + n_tm) % n_tm}
    below = {"tm": ((x + n_x - 1) % n_x) * 4 + tm % 4}
    above = {"tm": ((x + 1) % n_x) * 4 + tm % 4}
    mates = (
        {"tm": ((x + 1 - 2 * parity + n_x) % n_x) * 4 + tm % 4},
        {"tm": ((x - 1 + 2 * parity + n_x) % n_x) * 4 + tm % 4},
    )

    barrier = pltpu.get_barrier_semaphore()
    peers = [partner, far, below, above] + [{"head": (z + d) % n_head} for d in range(1, n_head)]
    for peer in peers:
        pl.semaphore_signal(barrier, inc=1, device_id=peer, device_id_type=MESH)

    def own_weight(h):
        return pltpu.make_async_copy(
            w_hbm.at[pl.ds(h * HD, HD)], wbuf.at[h, z], loc_sem.at[h])

    def own_kv(h):
        columns = pl.ds(h * HD, HD)
        return [
            pltpu.make_async_copy(k_hbm.at[:, :, columns], kbufs[h].at[pl.ds(0, tiles)], loc_sem.at[n_local + 2 * h]),
            pltpu.make_async_copy(v_hbm.at[:, :, columns], vbufs[h].at[pl.ds(0, tiles)], loc_sem.at[n_local + 2 * h + 1]),
        ]

    own_q = pltpu.make_async_copy(q_hbm, qbuf, loc_sem.at[3 * n_local])
    for h in range(n_local):
        own_weight(h).start()
    own_q.start()
    for h in range(n_local):
        for copy in own_kv(h):
            copy.start()

    def kv_send(h, slab, to, send, recv):
        columns = pl.ds(h * HD, HD)
        rows = pl.ds(slab * tiles, tiles)
        return [
            pltpu.make_async_remote_copy(
                src_ref=src.at[:, :, columns], dst_ref=dst.at[rows], send_sem=send.at[2 * h + i],
                recv_sem=recv.at[2 * h + i], device_id=to, device_id_type=MESH)
            for i, (src, dst) in enumerate(((k_hbm, kbufs[h]), (v_hbm, vbufs[h])))
        ]

    def far_copies(h):
        return kv_send(h, 2, far, halo_send, halo_recv)

    def core_copies(h):
        return kv_send(h, 1, partner, core_send, core_recv)

    def piece(h, block, ring, rows):
        return wbuf.at[h, block, rows, pl.ds(core * half + ring * quarter, quarter)]

    my_rows = pl.ds(parity * (HD // 2), HD // 2)

    def ring_copy(h, s, ring):
        sign = 1 - 2 * ring
        ref = piece(h, (z - sign * s + n_head) % n_head, ring, my_rows)
        return pltpu.make_async_remote_copy(
            src_ref=ref, dst_ref=ref, send_sem=ring_send.at[h, s, ring], recv_sem=ring_recv.at[h, s, ring],
            device_id={"head": (z + sign + n_head) % n_head}, device_id_type=MESH)

    def mate_copy(h, s, ring):
        sign = 1 - 2 * ring
        ref = piece(h, (z - sign * (s + 1) + 2 * n_head) % n_head, ring, my_rows)
        return pltpu.make_async_remote_copy(
            src_ref=ref, dst_ref=ref, send_sem=mate_send.at[h, s, ring], recv_sem=mate_recv.at[h, s, ring],
            device_id=mates[ring], device_id_type=MESH)

    def pair_copy(h, s, ring):
        sign = 1 - 2 * ring
        ref = piece(h, (z - sign * (s + 1) + 2 * n_head) % n_head, ring, pl.ds(0, HD))
        return pltpu.make_async_remote_copy(
            src_ref=ref, dst_ref=ref, send_sem=pair_send.at[h, s, ring], recv_sem=pair_recv.at[h, s, ring],
            device_id=partner, device_id_type=MESH)

    hops = n_head - 1

    def tick(t):
        for h in range(n_local):
            s = t - STAGGER * h
            for ring in range(2):
                if s == 0:
                    if ring == 0:
                        own_weight(h).wait()
                    ring_copy(h, 0, ring).start()
                if 1 <= s <= hops:
                    ring_copy(h, s - 1, ring).wait_recv()
                    if s < hops:
                        ring_copy(h, s, ring).start()
                    mate_copy(h, s - 1, ring).start()
            for ring in range(2):
                if 2 <= s <= hops + 1:
                    mate_copy(h, s - 2, ring).wait_recv()
                    pair_copy(h, s - 2, ring).start()

    ticks = STAGGER * (n_local - 1) + hops + 2

    factor = math.log2(math.e) / math.sqrt(HD)
    slot_of = lax.broadcasted_iota(jnp.int32, (1, SLOTS * TILE), 1) // TILE

    def a2a_copy(h, d):
        to = (z + d) % n_head
        return pltpu.make_async_remote_copy(
            src_ref=att.at[h, pl.ds(pl.multiple_of(to * TILE, TILE), TILE)],
            dst_ref=arecv.at[h, :, pl.ds(pl.multiple_of(z * HD, HD), HD)],
            send_sem=a_send.at[h, d], recv_sem=a_recv.at[h, d],
            device_id={"head": to}, device_id_type=MESH)

    def attend(h):
        kbuf, vbuf = kbufs[h], vbufs[h]

        def one_tile(step, carry):
            i = (z + 1 + step) % tiles
            i_h, i_w = i // NTW, i % NTW
            rows = pl.ds(pl.multiple_of(i * TILE, TILE), TILE)
            bias = jnp.zeros((1, SLOTS * TILE), jnp.float32)
            k_parts, v_parts = [], []
            for j in range(SLOTS):
                d_t, d_h, d_w = window[i, j, 0], window[i, j, 1], window[i, j, 2]
                t_j, h_j, w_j = tm + d_t, i_h + d_h, i_w + d_w
                valid = ((t_j >= 0) & (t_j < n_tm) & (h_j >= 0) & (h_j < NTH)
                         & (w_j >= 0) & (w_j < NTW))
                toward = d_t * (1 - 2 * core)
                slab = jnp.where(toward == 0, 0, jnp.where(toward == 1, 1, 2))
                index = jnp.where(valid, slab * tiles + h_j * NTW + w_j, i)
                bias = jnp.where(slot_of == j, jnp.where(valid, 0.0, NEG), bias)
                k_parts.append(kbuf[index])
                v_parts.append(vbuf[index])
            q = qbuf[rows, h * HD:(h + 1) * HD]
            scores = lax.dot_general(
                q, jnp.concatenate(k_parts, axis=0), (((1,), (1,)), ((), ())),
                preferred_element_type=jnp.float32) + bias
            top = jnp.max(scores, axis=1, keepdims=True)
            weights = jnp.exp2((scores - top) * factor)
            total = jnp.sum(weights, axis=1, keepdims=True)
            mixed = jnp.dot(weights.astype(jnp.bfloat16), jnp.concatenate(v_parts, axis=0),
                            preferred_element_type=jnp.float32)
            att[h, rows, :] = (mixed / total).astype(jnp.bfloat16)

            @pl.when(step < tiles - 1)
            def _():
                a2a_copy(h, step + 1).start()
            return carry

        lax.fori_loop(0, tiles, one_tile, 0)
        own_rows = pl.ds(pl.multiple_of(z * TILE, TILE), TILE)
        own_columns = pl.ds(pl.multiple_of(z * HD, HD), HD)
        arecv[h, :, own_columns] = att[h, own_rows, :]

    block = 512

    def out_copy(n):
        columns = pl.ds(n * block, block)
        return pltpu.make_async_copy(acc.at[:, columns], out_hbm.at[:, columns], out_sem.at[n])

    def project(h):
        for s in range(hops):
            for ring in range(2):
                pair_copy(h, s, ring).wait_recv()
        for d in range(1, n_head):
            a2a_copy(h, d).wait_recv()
        lhs = arecv[h]
        for n in range(width // block):
            columns = slice(n * block, (n + 1) * block)
            rhs = wbuf[h, :, :, columns].reshape(n_head * HD, block)
            term = jnp.dot(lhs, rhs, preferred_element_type=jnp.float32)
            acc[:, columns] = term if h == 0 else acc[:, columns] + term
            if h == n_local - 1:
                out_copy(n).start()

    pl.semaphore_wait(barrier, len(peers))
    for h in range(n_local):
        if h == 0:
            for copy in far_copies(h):
                copy.start()
    for h in range(n_local):
        for copy in core_copies(h):
            copy.start()

    attend_after = ATTEND_AFTER
    project_after = PROJECT_AFTER
    for t in range(ticks):
        tick(t)
        for h in range(n_local):
            if attend_after[h] == t:
                for copy in far_copies(h) + core_copies(h):
                    copy.wait_recv()
                if h + 1 < n_local:
                    for copy in far_copies(h + 1):
                        copy.start()
                for copy in own_kv(h):
                    copy.wait()
                if h == 0:
                    own_q.wait()
                attend(h)
            if project_after[h] == t:
                project(h)
    for h in range(n_local):
        for copy in far_copies(h) + core_copies(h):
            copy.wait_send()
        for d in range(1, n_head):
            a2a_copy(h, d).wait_send()
        for s in range(hops):
            for ring in range(2):
                ring_copy(h, s, ring).wait_send()
                mate_copy(h, s, ring).wait_send()
                pair_copy(h, s, ring).wait_send()
    for n in range(width // block):
        out_copy(n).wait()


ATTEND_AFTER = (4, 9, 13)
PROJECT_AFTER = (11, 15, 16)


def by_tile(rows):
    return rows.reshape(rows.shape[0] // TILE, TILE, rows.shape[1])


def body(queries, key_rows, values, out_weight, gate_scale, window):
    n_tm, n_head = lax.axis_size("tm"), lax.axis_size("head")
    tokens, features = queries.shape
    n_local = features // HD
    width = out_weight.shape[1]
    hops = n_head - 1
    dma = pltpu.SemaphoreType.DMA
    any_spec = pl.BlockSpec(memory_space=pl.ANY)
    projected = pl.pallas_call(
        functools.partial(kernel, n_tm, n_head, n_local),
        out_shape=jax.ShapeDtypeStruct((tokens // n_head, width), jnp.float32),
        in_specs=[any_spec] * 4 + [pl.BlockSpec(memory_space=pltpu.SMEM)],
        out_specs=any_spec,
        scratch_shapes=[
            pltpu.VMEM((tokens, features), jnp.bfloat16),
            pltpu.VMEM((n_local, tokens, HD), jnp.bfloat16),
            pltpu.VMEM((n_local, TILE, n_head * HD), jnp.bfloat16),
            pltpu.VMEM((n_local, n_head, HD, width), jnp.bfloat16),
            pltpu.VMEM((tokens // n_head, width), jnp.float32),
        ] + [pltpu.VMEM((3 * tokens // TILE, TILE, HD), jnp.bfloat16)] * (2 * n_local) + [
            dma((3 * n_local + 1,)), dma((width // 512,)),
            dma((2 * n_local,)), dma((2 * n_local,)), dma((2 * n_local,)), dma((2 * n_local,)),
            dma((n_local, n_head)), dma((n_local, n_head)),
            dma((n_local, hops, 2)), dma((n_local, hops, 2)),
            dma((n_local, hops, 2)), dma((n_local, hops, 2)),
            dma((n_local, hops, 2)), dma((n_local, hops, 2)),
        ],
        compiler_params=pltpu.CompilerParams(
            collective_id=0, has_side_effects=True, vmem_limit_bytes=56 << 20),
        name="attend_and_project",
    )(queries, by_tile(key_rows), by_tile(values), out_weight, window)
    return gate_scale[None, :] * projected


def solution(mesh):
    placed = (
        P(("prompt", "tm"), "head"),
        P(("prompt", "tm"), "head"),
        P(("prompt", "tm"), "head"),
        P("head", None),
        P("prompt"),
        P(("prompt", "tm"), None, None),
    )
    return jax.shard_map(
        body,
        mesh=mesh,
        in_specs=placed,
        out_specs=P(("prompt", "tm", "head"), None),
        check_vma=False,
    )
```

```python
import functools
import math

import jax
import jax.numpy as jnp
from jax import lax
from jax.experimental import pallas as pl
from jax.experimental.pallas import tpu as pltpu
from jax.sharding import PartitionSpec as P

HD = 128
TILE = 192
NTH = 2
NTW = 4
SLOTS = 8
MESH = pl.DeviceIdType.MESH
NEG = -1e30
VMEM_LIMIT = 56
FEW = 48
BUSY = 1


def kernel(n_tm, n_head, n_local, q_hbm, k_hbm, v_hbm, w_hbm, window, out,
           qbuf, att, arecv, wbuf, *rest):
    kbufs, vbufs = rest[:n_local], rest[n_local:2 * n_local]
    (loc_sem, halo_send, halo_recv, core_send, core_recv, a_send, a_recv,
     ring_send, ring_recv, mate_send, mate_recv, pair_send, pair_recv) = rest[2 * n_local:]
    tokens = q_hbm.shape[0]
    tiles = tokens // TILE
    width = w_hbm.shape[1]
    half, quarter = width // 2, width // 4

    tm = lax.axis_index("tm")
    z = lax.axis_index("head")
    core = tm % 2
    x = tm // 4
    n_x = n_tm // 4
    parity = x % 2
    partner = {"tm": tm + 1 - 2 * core}
    far = {"tm": (tm - 1 + 2 * core + n_tm) % n_tm}
    busy = (tm // 2 + BUSY + 1) % 2
    light, heavy = (
        {"tm": ((x + sign + n_x) % n_x) * 4 + tm % 4} for sign in (2 * busy - 1, 1 - 2 * busy))

    barrier = pltpu.get_barrier_semaphore()
    peers = [partner, far, light, heavy] + [{"head": (z + d) % n_head} for d in range(1, n_head)]
    for peer in peers:
        pl.semaphore_signal(barrier, inc=1, device_id=peer, device_id_type=MESH)

    def own_weight(h):
        return pltpu.make_async_copy(
            w_hbm.at[pl.ds(h * HD, HD)], wbuf.at[h, z], loc_sem.at[h])

    def own_kv(h):
        columns = pl.ds(h * HD, HD)
        return [
            pltpu.make_async_copy(k_hbm.at[:, :, columns], kbufs[h].at[pl.ds(0, tiles)], loc_sem.at[n_local + 2 * h]),
            pltpu.make_async_copy(v_hbm.at[:, :, columns], vbufs[h].at[pl.ds(0, tiles)], loc_sem.at[n_local + 2 * h + 1]),
        ]

    own_q = pltpu.make_async_copy(q_hbm, qbuf, loc_sem.at[3 * n_local])
    for h in range(n_local):
        own_weight(h).start()
    own_q.start()
    for h in range(n_local):
        for copy in own_kv(h):
            copy.start()

    def kv_send(h, slab, to, send, recv):
        columns = pl.ds(h * HD, HD)
        rows = pl.ds(slab * tiles, tiles)
        return [
            pltpu.make_async_remote_copy(
                src_ref=src.at[:, :, columns], dst_ref=dst.at[rows], send_sem=send.at[2 * h + i],
                recv_sem=recv.at[2 * h + i], device_id=to, device_id_type=MESH)
            for i, (src, dst) in enumerate(((k_hbm, kbufs[h]), (v_hbm, vbufs[h])))
        ]

    def far_copies(h):
        return kv_send(h, 2, far, halo_send, halo_recv)

    def core_copies(h):
        return kv_send(h, 1, partner, core_send, core_recv)

    counts = (FEW, HD - FEW)
    parts = ((parity + 1 - busy) % 2, (parity + busy) % 2)
    firsts = ((1 - busy) * (HD - FEW), busy * FEW)
    hops = n_head // 2

    def block_of(s, ring):
        return (z - (1 - 2 * ring) * s + n_head) % n_head

    def piece(h, block, kind):
        return wbuf.at[h, block, pl.ds(pl.multiple_of(firsts[kind], 16), counts[kind]),
                       pl.ds(pl.multiple_of(core * half + parts[kind] * quarter, HD), quarter)]

    def kinds(h, s, ring):
        return range(2) if s < hops - 1 else ((h + ring) % 2,)

    def ring_copies(h, s, ring):
        copies = []
        for kind in kinds(h, s, ring):
            ref = piece(h, block_of(s, ring), kind)
            copies.append(pltpu.make_async_remote_copy(
                src_ref=ref, dst_ref=ref, send_sem=ring_send.at[h, s, ring, kind],
                recv_sem=ring_recv.at[h, s, ring, kind],
                device_id={"head": (z + 1 - 2 * ring + n_head) % n_head}, device_id_type=MESH))
        return copies

    def mate_copies(h, s, ring):
        copies = []
        for kind in kinds(h, s, ring):
            ref = piece(h, block_of(s + 1, ring), kind)
            copies.append(pltpu.make_async_remote_copy(
                src_ref=ref, dst_ref=ref, send_sem=mate_send.at[h, s, ring, kind],
                recv_sem=mate_recv.at[h, s, ring, kind], device_id=(light, heavy)[kind], device_id_type=MESH))
        return copies

    def pair_copy(h, s, ring):
        ref = wbuf.at[h, block_of(s + 1, ring), :, pl.ds(pl.multiple_of(core * half, HD), half)]
        return pltpu.make_async_remote_copy(
            src_ref=ref, dst_ref=ref, send_sem=pair_send.at[h, s, ring], recv_sem=pair_recv.at[h, s, ring],
            device_id=partner, device_id_type=MESH)

    received = [(s, ring) for s in range(hops - 1) for ring in range(2)] + [(hops - 1, 0)]

    def tick(s):
        for h in range(n_local):
            if s == 0:
                own_weight(h).wait()
            for ring in range(2):
                if 1 <= s <= hops:
                    for copy in ring_copies(h, s - 1, ring):
                        copy.wait_recv()
                if s < hops:
                    for copy in ring_copies(h, s, ring):
                        copy.start()
                if 1 <= s <= hops:
                    for copy in mate_copies(h, s - 1, ring):
                        copy.start()

    def share(s):
        for h in range(n_local):
            for ring in range(2):
                for copy in mate_copies(h, s, ring):
                    copy.wait_recv()
                if s < hops - 1:
                    pair_copy(h, s, ring).start()
            if s == hops - 1:
                pair_copy(h, s, 0).start()

    factor = math.log2(math.e) / math.sqrt(HD)
    slot_of = lax.broadcasted_iota(jnp.int32, (1, SLOTS * TILE), 1) // TILE

    def a2a_copy(h, d):
        to = (z + d) % n_head
        return pltpu.make_async_remote_copy(
            src_ref=att.at[h, pl.ds(pl.multiple_of(to * TILE, TILE), TILE)],
            dst_ref=arecv.at[h, :, pl.ds(pl.multiple_of(z * HD, HD), HD)],
            send_sem=a_send.at[h, d], recv_sem=a_recv.at[h, d],
            device_id={"head": to}, device_id_type=MESH)

    def attend(h):
        kbuf, vbuf = kbufs[h], vbufs[h]

        def one_tile(step, carry):
            i = (z + 1 + step) % tiles
            i_h, i_w = i // NTW, i % NTW
            rows = pl.ds(pl.multiple_of(i * TILE, TILE), TILE)
            bias = jnp.zeros((1, SLOTS * TILE), jnp.float32)
            k_parts, v_parts = [], []
            for j in range(SLOTS):
                d_t, d_h, d_w = window[0, i, j], window[1, i, j], window[2, i, j]
                t_j, h_j, w_j = tm + d_t, i_h + d_h, i_w + d_w
                valid = ((t_j >= 0) & (t_j < n_tm) & (h_j >= 0) & (h_j < NTH)
                         & (w_j >= 0) & (w_j < NTW))
                toward = d_t * (1 - 2 * core)
                slab = jnp.where(toward == 0, 0, jnp.where(toward == 1, 1, 2))
                index = jnp.where(valid, slab * tiles + h_j * NTW + w_j, i)
                bias = jnp.where(slot_of == j, jnp.where(valid, 0.0, NEG), bias)
                k_parts.append(kbuf[index])
                v_parts.append(vbuf[index])
            q = qbuf[rows, h * HD:(h + 1) * HD]
            scores = lax.dot_general(
                q, jnp.concatenate(k_parts, axis=0), (((1,), (1,)), ((), ())),
                preferred_element_type=jnp.float32) + bias
            top = jnp.max(scores, axis=1, keepdims=True)
            weights = jnp.exp2((scores - top) * factor)
            total = jnp.sum(weights, axis=1, keepdims=True)
            mixed = jnp.dot(weights.astype(jnp.bfloat16), jnp.concatenate(v_parts, axis=0),
                            preferred_element_type=jnp.float32)
            att[h, rows, :] = (mixed / total).astype(jnp.bfloat16)

            @pl.when(step < tiles - 1)
            def _():
                a2a_copy(h, step + 1).start()
            return carry

        lax.fori_loop(0, tiles, one_tile, 0)
        own_rows = pl.ds(pl.multiple_of(z * TILE, TILE), TILE)
        own_columns = pl.ds(pl.multiple_of(z * HD, HD), HD)
        arecv[h, :, own_columns] = att[h, own_rows, :]

    block = 512

    def project(h):
        for s, ring in received:
            pair_copy(h, s, ring).wait_recv()
        for d in range(1, n_head):
            a2a_copy(h, d).wait_recv()
        lhs = arecv[h]
        for n in range(width // block):
            columns = slice(n * block, (n + 1) * block)
            rhs = wbuf[h, :, :, columns].reshape(n_head * HD, block)
            term = jnp.dot(lhs, rhs, preferred_element_type=jnp.float32)
            out[:, columns] = term if h == 0 else out[:, columns] + term

    def start_attend(h):
        for copy in far_copies(h) + core_copies(h):
            copy.wait_recv()
        for copy in own_kv(h):
            copy.wait()
        attend(h)

    pl.semaphore_wait(barrier, len(peers))
    for h in range(n_local - 1):
        for copy in far_copies(h):
            copy.start()
    tick(0)
    for h in range(n_local):
        for copy in core_copies(h):
            copy.start()
    own_q.wait()
    for step in ORDER:
        what, which = step
        if what == "tick":
            tick(which)
        elif what == "share":
            share(which)
        elif what == "far":
            for copy in far_copies(which):
                copy.start()
        elif what == "attend":
            start_attend(which)
        elif what == "project":
            project(which)
    for h in range(n_local):
        for copy in far_copies(h) + core_copies(h):
            copy.wait_send()
        for d in range(1, n_head):
            a2a_copy(h, d).wait_send()
        for s in range(hops):
            for ring in range(2):
                for copy in ring_copies(h, s, ring) + mate_copies(h, s, ring):
                    copy.wait_send()
        for s, ring in received:
            pair_copy(h, s, ring).wait_send()


ORDER = (
    ("tick", 1), ("tick", 2), ("far", 2), ("share", 0), ("tick", 3), ("share", 1), ("attend", 0), ("tick", 4),
    ("attend", 1), ("share", 2), ("share", 3), ("project", 0), ("attend", 2), ("project", 1), ("project", 2),
)


def by_tile(rows):
    return rows.reshape(rows.shape[0] // TILE, TILE, rows.shape[1])


def body(queries, key_rows, values, out_weight, gate_scale, window):
    n_tm, n_head = lax.axis_size("tm"), lax.axis_size("head")
    tokens, features = queries.shape
    n_local = features // HD
    width = out_weight.shape[1]
    hops = n_head // 2
    dma = pltpu.SemaphoreType.DMA
    hbm_spec = pl.BlockSpec(memory_space=pltpu.HBM)
    projected = pl.pallas_call(
        functools.partial(kernel, n_tm, n_head, n_local),
        out_shape=jax.ShapeDtypeStruct((tokens // n_head, width), jnp.float32),
        in_specs=[hbm_spec] * 4 + [pl.BlockSpec(memory_space=pltpu.SMEM)],
        out_specs=pl.BlockSpec(memory_space=pltpu.VMEM),
        scratch_shapes=[
            pltpu.VMEM((tokens, features), jnp.bfloat16),
            pltpu.VMEM((n_local, tokens, HD), jnp.bfloat16),
            pltpu.VMEM((n_local, TILE, n_head * HD), jnp.bfloat16),
            pltpu.VMEM((n_local, n_head, HD, width), jnp.bfloat16),
        ] + [pltpu.VMEM((3 * tokens // TILE, TILE, HD), jnp.bfloat16)] * (2 * n_local) + [
            dma((3 * n_local + 1,)),
            dma((2 * n_local,)), dma((2 * n_local,)), dma((2 * n_local,)), dma((2 * n_local,)),
            dma((n_local, n_head)), dma((n_local, n_head)),
            dma((n_local, hops, 2, 2)), dma((n_local, hops, 2, 2)),
            dma((n_local, hops, 2, 2)), dma((n_local, hops, 2, 2)),
            dma((n_local, hops, 2)), dma((n_local, hops, 2)),
        ],
        compiler_params=pltpu.CompilerParams(
            collective_id=0, has_side_effects=True, vmem_limit_bytes=VMEM_LIMIT << 20),
        name="attend_and_project",
    )(queries, by_tile(key_rows), by_tile(values), out_weight, window.transpose(2, 0, 1))
    return gate_scale[None, :] * projected


def solution(mesh):
    placed = (
        P(("prompt", "tm"), "head"),
        P(("prompt", "tm"), "head"),
        P(("prompt", "tm"), "head"),
        P("head", None),
        P("prompt"),
        P(("prompt", "tm"), None, None),
    )
    return jax.shard_map(
        body,
        mesh=mesh,
        in_specs=placed,
        out_specs=P(("prompt", "tm", "head"), None),
        check_vma=False,
    )
```

```python
import functools
import math

import jax
import jax.numpy as jnp
from jax import lax
from jax.experimental import pallas as pl
from jax.experimental.pallas import tpu as pltpu
from jax.sharding import PartitionSpec as P

HD = 128
TILE = 192
NTH = 2
NTW = 4
SLOTS = 8
MESH = pl.DeviceIdType.MESH
NEG = -1e30
VMEM_LIMIT = 56
FEW = 48
BUSY = 1


def kernel(n_tm, n_head, n_local, q_hbm, k_hbm, v_hbm, w_hbm, window, out_hbm,
           qbuf, att, arecv, wbuf, out, *rest):
    kbufs, vbufs = rest[:n_local], rest[n_local:2 * n_local]
    (loc_sem, out_sem, halo_send, halo_recv, core_send, core_recv, a_send, a_recv,
     ring_send, ring_recv, mate_send, mate_recv, pair_send, pair_recv) = rest[2 * n_local:]
    tokens = q_hbm.shape[0]
    tiles = tokens // TILE
    width = w_hbm.shape[1]
    half, quarter = width // 2, width // 4

    tm = lax.axis_index("tm")
    z = lax.axis_index("head")
    core = tm % 2
    x = tm // 4
    n_x = n_tm // 4
    parity = x % 2
    partner = {"tm": tm + 1 - 2 * core}
    far = {"tm": (tm - 1 + 2 * core + n_tm) % n_tm}
    busy = (tm // 2 + BUSY + 1) % 2
    light, heavy = (
        {"tm": ((x + sign + n_x) % n_x) * 4 + tm % 4} for sign in (2 * busy - 1, 1 - 2 * busy))

    barrier = pltpu.get_barrier_semaphore()
    peers = [partner, far, light, heavy] + [{"head": (z + d) % n_head} for d in range(1, n_head)]
    for peer in peers:
        pl.semaphore_signal(barrier, inc=1, device_id=peer, device_id_type=MESH)

    def own_weight(h):
        return pltpu.make_async_copy(
            w_hbm.at[pl.ds(h * HD, HD)], wbuf.at[h, z], loc_sem.at[h])

    def own_kv(h):
        columns = pl.ds(h * HD, HD)
        return [
            pltpu.make_async_copy(k_hbm.at[:, :, columns], kbufs[h].at[pl.ds(0, tiles)], loc_sem.at[n_local + 2 * h]),
            pltpu.make_async_copy(v_hbm.at[:, :, columns], vbufs[h].at[pl.ds(0, tiles)], loc_sem.at[n_local + 2 * h + 1]),
        ]

    own_q = pltpu.make_async_copy(q_hbm, qbuf, loc_sem.at[3 * n_local])
    for h in range(n_local):
        own_weight(h).start()
    own_q.start()
    for h in range(n_local):
        for copy in own_kv(h):
            copy.start()

    def kv_send(h, slab, to, send, recv):
        columns = pl.ds(h * HD, HD)
        rows = pl.ds(slab * tiles, tiles)
        return [
            pltpu.make_async_remote_copy(
                src_ref=src.at[:, :, columns], dst_ref=dst.at[rows], send_sem=send.at[2 * h + i],
                recv_sem=recv.at[2 * h + i], device_id=to, device_id_type=MESH)
            for i, (src, dst) in enumerate(((k_hbm, kbufs[h]), (v_hbm, vbufs[h])))
        ]

    def far_copies(h):
        return kv_send(h, 2, far, halo_send, halo_recv)

    def core_copies(h):
        return kv_send(h, 1, partner, core_send, core_recv)

    counts = (FEW, HD - FEW)
    parts = ((parity + 1 - busy) % 2, (parity + busy) % 2)
    firsts = ((1 - busy) * (HD - FEW), busy * FEW)
    hops = n_head // 2

    def block_of(s, ring):
        return (z - (1 - 2 * ring) * s + n_head) % n_head

    def piece(h, block, kind):
        return wbuf.at[h, block, pl.ds(pl.multiple_of(firsts[kind], 16), counts[kind]),
                       pl.ds(pl.multiple_of(core * half + parts[kind] * quarter, HD), quarter)]

    def kinds(h, s, ring):
        return range(2) if s < hops - 1 else ((h + ring) % 2,)

    def ring_copies(h, s, ring):
        copies = []
        for kind in kinds(h, s, ring):
            ref = piece(h, block_of(s, ring), kind)
            copies.append(pltpu.make_async_remote_copy(
                src_ref=ref, dst_ref=ref, send_sem=ring_send.at[h, s, ring, kind],
                recv_sem=ring_recv.at[h, s, ring, kind],
                device_id={"head": (z + 1 - 2 * ring + n_head) % n_head}, device_id_type=MESH))
        return copies

    def mate_copies(h, s, ring):
        copies = []
        for kind in kinds(h, s, ring):
            ref = piece(h, block_of(s + 1, ring), kind)
            copies.append(pltpu.make_async_remote_copy(
                src_ref=ref, dst_ref=ref, send_sem=mate_send.at[h, s, ring, kind],
                recv_sem=mate_recv.at[h, s, ring, kind], device_id=(light, heavy)[kind], device_id_type=MESH))
        return copies

    def pair_copy(h, s, ring):
        ref = wbuf.at[h, block_of(s + 1, ring), :, pl.ds(pl.multiple_of(core * half, HD), half)]
        return pltpu.make_async_remote_copy(
            src_ref=ref, dst_ref=ref, send_sem=pair_send.at[h, s, ring], recv_sem=pair_recv.at[h, s, ring],
            device_id=partner, device_id_type=MESH)

    received = [(s, ring) for s in range(hops - 1) for ring in range(2)] + [(hops - 1, 0)]

    def tick(s):
        for h in range(n_local):
            if s == 0:
                own_weight(h).wait()
            for ring in range(2):
                if 1 <= s <= hops:
                    for copy in ring_copies(h, s - 1, ring):
                        copy.wait_recv()
                if s < hops:
                    for copy in ring_copies(h, s, ring):
                        copy.start()
                if 1 <= s <= hops:
                    for copy in mate_copies(h, s - 1, ring):
                        copy.start()

    def share(s):
        for h in range(n_local):
            for ring in range(2):
                for copy in mate_copies(h, s, ring):
                    copy.wait_recv()
                if s < hops - 1:
                    pair_copy(h, s, ring).start()
            if s == hops - 1:
                pair_copy(h, s, 0).start()

    factor = math.log2(math.e) / math.sqrt(HD)
    slot_of = lax.broadcasted_iota(jnp.int32, (1, SLOTS * TILE), 1) // TILE

    def a2a_copy(h, d):
        to = (z + d) % n_head
        return pltpu.make_async_remote_copy(
            src_ref=att.at[h, pl.ds(pl.multiple_of(to * TILE, TILE), TILE)],
            dst_ref=arecv.at[h, :, pl.ds(pl.multiple_of(z * HD, HD), HD)],
            send_sem=a_send.at[h, d], recv_sem=a_recv.at[h, d],
            device_id={"head": to}, device_id_type=MESH)

    def attend(h):
        kbuf, vbuf = kbufs[h], vbufs[h]

        def one_tile(step, carry):
            i = (z + 1 + step) % tiles
            i_h, i_w = i // NTW, i % NTW
            rows = pl.ds(pl.multiple_of(i * TILE, TILE), TILE)
            bias = jnp.zeros((1, SLOTS * TILE), jnp.float32)
            k_parts, v_parts = [], []
            for j in range(SLOTS):
                d_t, d_h, d_w = window[0, i, j], window[1, i, j], window[2, i, j]
                t_j, h_j, w_j = tm + d_t, i_h + d_h, i_w + d_w
                valid = ((t_j >= 0) & (t_j < n_tm) & (h_j >= 0) & (h_j < NTH)
                         & (w_j >= 0) & (w_j < NTW))
                toward = d_t * (1 - 2 * core)
                slab = jnp.where(toward == 0, 0, jnp.where(toward == 1, 1, 2))
                index = jnp.where(valid, slab * tiles + h_j * NTW + w_j, i)
                bias = jnp.where(slot_of == j, jnp.where(valid, 0.0, NEG), bias)
                k_parts.append(kbuf[index])
                v_parts.append(vbuf[index])
            q = qbuf[rows, h * HD:(h + 1) * HD]
            scores = lax.dot_general(
                q, jnp.concatenate(k_parts, axis=0), (((1,), (1,)), ((), ())),
                preferred_element_type=jnp.float32) + bias
            top = jnp.max(scores, axis=1, keepdims=True)
            weights = jnp.exp2((scores - top) * factor)
            total = jnp.sum(weights, axis=1, keepdims=True)
            mixed = jnp.dot(weights.astype(jnp.bfloat16), jnp.concatenate(v_parts, axis=0),
                            preferred_element_type=jnp.float32)
            att[h, rows, :] = (mixed / total).astype(jnp.bfloat16)

            @pl.when(step < tiles - 1)
            def _():
                a2a_copy(h, step + 1).start()
            return carry

        lax.fori_loop(0, tiles, one_tile, 0)
        own_rows = pl.ds(pl.multiple_of(z * TILE, TILE), TILE)
        own_columns = pl.ds(pl.multiple_of(z * HD, HD), HD)
        arecv[h, :, own_columns] = att[h, own_rows, :]

    block = 512

    def out_copy(n):
        columns = pl.ds(n * block, block)
        return pltpu.make_async_copy(out.at[:, columns], out_hbm.at[:, columns], out_sem.at[n])

    def project(h):
        for s, ring in received:
            pair_copy(h, s, ring).wait_recv()
        for d in range(1, n_head):
            a2a_copy(h, d).wait_recv()
        lhs = arecv[h]
        for n in range(width // block):
            columns = slice(n * block, (n + 1) * block)
            rhs = wbuf[h, :, :, columns].reshape(n_head * HD, block)
            term = jnp.dot(lhs, rhs, preferred_element_type=jnp.float32)
            out[:, columns] = term if h == 0 else out[:, columns] + term
            if h == n_local - 1:
                out_copy(n).start()

    def start_attend(h):
        for copy in far_copies(h) + core_copies(h):
            copy.wait_recv()
        for copy in own_kv(h):
            copy.wait()
        attend(h)

    pl.semaphore_wait(barrier, len(peers))
    for h in range(n_local - 1):
        for copy in far_copies(h):
            copy.start()
    tick(0)
    for h in range(n_local):
        for copy in core_copies(h):
            copy.start()
    own_q.wait()
    for step in ORDER:
        what, which = step
        if what == "tick":
            tick(which)
        elif what == "share":
            share(which)
        elif what == "far":
            for copy in far_copies(which):
                copy.start()
        elif what == "attend":
            start_attend(which)
        elif what == "project":
            project(which)
    for h in range(n_local):
        for copy in far_copies(h) + core_copies(h):
            copy.wait_send()
        for d in range(1, n_head):
            a2a_copy(h, d).wait_send()
        for s in range(hops):
            for ring in range(2):
                for copy in ring_copies(h, s, ring) + mate_copies(h, s, ring):
                    copy.wait_send()
        for s, ring in received:
            pair_copy(h, s, ring).wait_send()
    for n in range(width // block):
        out_copy(n).wait()


ORDER = (
    ("tick", 1), ("tick", 2), ("far", 2), ("share", 0), ("tick", 3), ("attend", 0), ("share", 1), ("tick", 4),
    ("attend", 1), ("share", 2), ("share", 3), ("attend", 2), ("project", 0), ("project", 1), ("project", 2),
)


def by_tile(rows):
    return rows.reshape(rows.shape[0] // TILE, TILE, rows.shape[1])


def body(queries, key_rows, values, out_weight, gate_scale, window):
    n_tm, n_head = lax.axis_size("tm"), lax.axis_size("head")
    tokens, features = queries.shape
    n_local = features // HD
    width = out_weight.shape[1]
    hops = n_head // 2
    dma = pltpu.SemaphoreType.DMA
    hbm_spec = pl.BlockSpec(memory_space=pltpu.HBM)
    projected = pl.pallas_call(
        functools.partial(kernel, n_tm, n_head, n_local),
        out_shape=jax.ShapeDtypeStruct((tokens // n_head, width), jnp.float32),
        in_specs=[hbm_spec] * 4 + [pl.BlockSpec(memory_space=pltpu.SMEM)],
        out_specs=hbm_spec,
        scratch_shapes=[
            pltpu.VMEM((tokens, features), jnp.bfloat16),
            pltpu.VMEM((n_local, tokens, HD), jnp.bfloat16),
            pltpu.VMEM((n_local, TILE, n_head * HD), jnp.bfloat16),
            pltpu.VMEM((n_local, n_head, HD, width), jnp.bfloat16),
            pltpu.VMEM((tokens // n_head, width), jnp.float32),
        ] + [pltpu.VMEM((3 * tokens // TILE, TILE, HD), jnp.bfloat16)] * (2 * n_local) + [
            dma((3 * n_local + 1,)), dma((width // 512,)),
            dma((2 * n_local,)), dma((2 * n_local,)), dma((2 * n_local,)), dma((2 * n_local,)),
            dma((n_local, n_head)), dma((n_local, n_head)),
            dma((n_local, hops, 2, 2)), dma((n_local, hops, 2, 2)),
            dma((n_local, hops, 2, 2)), dma((n_local, hops, 2, 2)),
            dma((n_local, hops, 2)), dma((n_local, hops, 2)),
        ],
        compiler_params=pltpu.CompilerParams(
            collective_id=0, has_side_effects=True, vmem_limit_bytes=VMEM_LIMIT << 20),
        name="attend_and_project",
    )(queries, by_tile(key_rows), by_tile(values), out_weight, window.transpose(2, 0, 1))
    return gate_scale[None, :] * projected


def solution(mesh):
    placed = (
        P(("prompt", "tm"), "head"),
        P(("prompt", "tm"), "head"),
        P(("prompt", "tm"), "head"),
        P("head", None),
        P("prompt"),
        P(("prompt", "tm"), None, None),
    )
    return jax.shard_map(
        body,
        mesh=mesh,
        in_specs=placed,
        out_specs=P(("prompt", "tm", "head"), None),
        check_vma=False,
    )
```

```python
import functools
import math

import jax
import jax.numpy as jnp
from jax import lax
from jax.experimental import pallas as pl
from jax.experimental.pallas import tpu as pltpu
from jax.sharding import PartitionSpec as P

HD = 128
TILE = 192
NTH = 2
NTW = 4
SLOTS = 8
MESH = pl.DeviceIdType.MESH
NEG = -1e30
VMEM_LIMIT = 56
FEW = 48
BUSY = 1


def kernel(n_tm, n_head, n_local, q_hbm, k_hbm, v_hbm, w_hbm, window, out_hbm,
           qbuf, att, arecv, wbuf, out, *rest):
    kbufs, vbufs = rest[:n_local], rest[n_local:2 * n_local]
    (loc_sem, out_sem, halo_send, halo_recv, core_send, core_recv, a_send, a_recv,
     ring_send, ring_recv, mate_send, mate_recv, pair_send, pair_recv) = rest[2 * n_local:]
    tokens = q_hbm.shape[0]
    tiles = tokens // TILE
    width = w_hbm.shape[1]
    half, quarter = width // 2, width // 4

    tm = lax.axis_index("tm")
    z = lax.axis_index("head")
    core = tm % 2
    x = tm // 4
    n_x = n_tm // 4
    parity = x % 2
    partner = {"tm": tm + 1 - 2 * core}
    far = {"tm": (tm - 1 + 2 * core + n_tm) % n_tm}
    busy = (tm // 2 + BUSY + 1) % 2
    light, heavy = (
        {"tm": ((x + sign + n_x) % n_x) * 4 + tm % 4} for sign in (2 * busy - 1, 1 - 2 * busy))

    barrier = pltpu.get_barrier_semaphore()
    peers = [partner, far, light, heavy] + [{"head": (z + d) % n_head} for d in range(1, n_head)]
    for peer in peers:
        pl.semaphore_signal(barrier, inc=1, device_id=peer, device_id_type=MESH)

    def own_weight(h):
        return pltpu.make_async_copy(
            w_hbm.at[pl.ds(h * HD, HD)], wbuf.at[h, z], loc_sem.at[h])

    def own_kv(h):
        columns = pl.ds(h * HD, HD)
        return [
            pltpu.make_async_copy(k_hbm.at[:, :, columns], kbufs[h].at[pl.ds(0, tiles)], loc_sem.at[n_local + 2 * h]),
            pltpu.make_async_copy(v_hbm.at[:, :, columns], vbufs[h].at[pl.ds(0, tiles)], loc_sem.at[n_local + 2 * h + 1]),
        ]

    own_q = pltpu.make_async_copy(q_hbm, qbuf, loc_sem.at[3 * n_local])
    for h in range(n_local):
        own_weight(h).start()
    own_q.start()
    for h in range(n_local):
        for copy in own_kv(h):
            copy.start()

    def kv_send(h, slab, to, send, recv):
        columns = pl.ds(h * HD, HD)
        rows = pl.ds(slab * tiles, tiles)
        return [
            pltpu.make_async_remote_copy(
                src_ref=src.at[:, :, columns], dst_ref=dst.at[rows], send_sem=send.at[2 * h + i],
                recv_sem=recv.at[2 * h + i], device_id=to, device_id_type=MESH)
            for i, (src, dst) in enumerate(((k_hbm, kbufs[h]), (v_hbm, vbufs[h])))
        ]

    def far_copies(h):
        return kv_send(h, 2, far, halo_send, halo_recv)

    def core_copies(h):
        return kv_send(h, 1, partner, core_send, core_recv)

    counts = (FEW, HD - FEW)
    parts = ((parity + 1 - busy) % 2, (parity + busy) % 2)
    firsts = ((1 - busy) * (HD - FEW), busy * FEW)
    hops = n_head // 2

    def block_of(s, ring):
        return (z - (1 - 2 * ring) * s + n_head) % n_head

    def piece(h, block, kind):
        return wbuf.at[h, block, pl.ds(pl.multiple_of(firsts[kind], 16), counts[kind]),
                       pl.ds(pl.multiple_of(core * half + parts[kind] * quarter, HD), quarter)]

    def kinds(h, s, ring):
        return range(2) if s < hops - 1 else ((h + ring) % 2,)

    def ring_copies(h, s, ring):
        copies = []
        for kind in kinds(h, s, ring):
            ref = piece(h, block_of(s, ring), kind)
            copies.append(pltpu.make_async_remote_copy(
                src_ref=ref, dst_ref=ref, send_sem=ring_send.at[h, s, ring, kind],
                recv_sem=ring_recv.at[h, s, ring, kind],
                device_id={"head": (z + 1 - 2 * ring + n_head) % n_head}, device_id_type=MESH))
        return copies

    def mate_copies(h, s, ring):
        copies = []
        for kind in kinds(h, s, ring):
            ref = piece(h, block_of(s + 1, ring), kind)
            copies.append(pltpu.make_async_remote_copy(
                src_ref=ref, dst_ref=ref, send_sem=mate_send.at[h, s, ring, kind],
                recv_sem=mate_recv.at[h, s, ring, kind], device_id=(light, heavy)[kind], device_id_type=MESH))
        return copies

    def pair_copy(h, s, ring):
        ref = wbuf.at[h, block_of(s + 1, ring), :, pl.ds(pl.multiple_of(core * half, HD), half)]
        return pltpu.make_async_remote_copy(
            src_ref=ref, dst_ref=ref, send_sem=pair_send.at[h, s, ring], recv_sem=pair_recv.at[h, s, ring],
            device_id=partner, device_id_type=MESH)

    received = [(s, ring) for s in range(hops - 1) for ring in range(2)] + [(hops - 1, 0)]

    def tick(s):
        for h in range(n_local):
            if s == 0:
                own_weight(h).wait()
            for ring in range(2):
                if 1 <= s <= hops:
                    for copy in ring_copies(h, s - 1, ring):
                        copy.wait_recv()
                if s < hops:
                    for copy in ring_copies(h, s, ring):
                        copy.start()
                if 1 <= s <= hops:
                    for copy in mate_copies(h, s - 1, ring):
                        copy.start()

    def share(s):
        for h in range(n_local):
            for ring in range(2):
                for copy in mate_copies(h, s, ring):
                    copy.wait_recv()
                if s < hops - 1:
                    pair_copy(h, s, ring).start()
            if s == hops - 1:
                pair_copy(h, s, 0).start()

    factor = math.log2(math.e) / math.sqrt(HD)
    slot_of = lax.broadcasted_iota(jnp.int32, (1, SLOTS * TILE), 1) // TILE

    def a2a_copy(h, d):
        to = (z + d) % n_head
        return pltpu.make_async_remote_copy(
            src_ref=att.at[h, pl.ds(pl.multiple_of(to * TILE, TILE), TILE)],
            dst_ref=arecv.at[h, :, pl.ds(pl.multiple_of(z * HD, HD), HD)],
            send_sem=a_send.at[h, d], recv_sem=a_recv.at[h, d],
            device_id={"head": to}, device_id_type=MESH)

    def attend(h):
        kbuf, vbuf = kbufs[h], vbufs[h]

        def one_tile(step, carry):
            d = hops + (step + 1) // 2 * (1 - 2 * (step % 2))
            i = (z + d) % tiles
            i_h, i_w = i // NTW, i % NTW
            rows = pl.ds(pl.multiple_of(i * TILE, TILE), TILE)
            bias = jnp.zeros((1, SLOTS * TILE), jnp.float32)
            k_parts, v_parts = [], []
            for j in range(SLOTS):
                d_t, d_h, d_w = window[0, i, j], window[1, i, j], window[2, i, j]
                t_j, h_j, w_j = tm + d_t, i_h + d_h, i_w + d_w
                valid = ((t_j >= 0) & (t_j < n_tm) & (h_j >= 0) & (h_j < NTH)
                         & (w_j >= 0) & (w_j < NTW))
                toward = d_t * (1 - 2 * core)
                slab = jnp.where(toward == 0, 0, jnp.where(toward == 1, 1, 2))
                index = jnp.where(valid, slab * tiles + h_j * NTW + w_j, i)
                bias = jnp.where(slot_of == j, jnp.where(valid, 0.0, NEG), bias)
                k_parts.append(kbuf[index])
                v_parts.append(vbuf[index])
            q = qbuf[rows, h * HD:(h + 1) * HD]
            scores = lax.dot_general(
                q, jnp.concatenate(k_parts, axis=0), (((1,), (1,)), ((), ())),
                preferred_element_type=jnp.float32) + bias
            top = jnp.max(scores, axis=1, keepdims=True)
            weights = jnp.exp2((scores - top) * factor)
            total = jnp.sum(weights, axis=1, keepdims=True)
            mixed = jnp.dot(weights.astype(jnp.bfloat16), jnp.concatenate(v_parts, axis=0),
                            preferred_element_type=jnp.float32)
            att[h, rows, :] = (mixed / total).astype(jnp.bfloat16)

            @pl.when(step < tiles - 1)
            def _():
                a2a_copy(h, d).start()
            return carry

        lax.fori_loop(0, tiles, one_tile, 0)
        own_rows = pl.ds(pl.multiple_of(z * TILE, TILE), TILE)
        own_columns = pl.ds(pl.multiple_of(z * HD, HD), HD)
        arecv[h, :, own_columns] = att[h, own_rows, :]

    block = 512

    def out_copy(n):
        columns = pl.ds(n * block, block)
        return pltpu.make_async_copy(out.at[:, columns], out_hbm.at[:, columns], out_sem.at[n])

    def project(h):
        for s, ring in received:
            pair_copy(h, s, ring).wait_recv()
        for d in range(1, n_head):
            a2a_copy(h, d).wait_recv()
        lhs = arecv[h]
        for n in range(width // block):
            columns = slice(n * block, (n + 1) * block)
            rhs = wbuf[h, :, :, columns].reshape(n_head * HD, block)
            term = jnp.dot(lhs, rhs, preferred_element_type=jnp.float32)
            out[:, columns] = term if h == 0 else out[:, columns] + term
            if h == n_local - 1:
                out_copy(n).start()

    def start_attend(h):
        for copy in far_copies(h) + core_copies(h):
            copy.wait_recv()
        for copy in own_kv(h):
            copy.wait()
        attend(h)

    pl.semaphore_wait(barrier, len(peers))
    for h in range(n_local - 1):
        for copy in far_copies(h):
            copy.start()
    tick(0)
    for h in range(n_local):
        for copy in core_copies(h):
            copy.start()
    own_q.wait()
    for step in ORDER:
        what, which = step
        if what == "tick":
            tick(which)
        elif what == "share":
            share(which)
        elif what == "far":
            for copy in far_copies(which):
                copy.start()
        elif what == "attend":
            start_attend(which)
        elif what == "project":
            project(which)
    for h in range(n_local):
        for copy in far_copies(h) + core_copies(h):
            copy.wait_send()
        for d in range(1, n_head):
            a2a_copy(h, d).wait_send()
        for s in range(hops):
            for ring in range(2):
                for copy in ring_copies(h, s, ring) + mate_copies(h, s, ring):
                    copy.wait_send()
        for s, ring in received:
            pair_copy(h, s, ring).wait_send()
    for n in range(width // block):
        out_copy(n).wait()


ORDER = (
    ("tick", 1), ("tick", 2), ("far", 2), ("share", 0), ("tick", 3), ("attend", 0), ("share", 1), ("tick", 4),
    ("attend", 1), ("share", 2), ("share", 3), ("attend", 2), ("project", 0), ("project", 1), ("project", 2),
)


def by_tile(rows):
    return rows.reshape(rows.shape[0] // TILE, TILE, rows.shape[1])


def body(queries, key_rows, values, out_weight, gate_scale, window):
    n_tm, n_head = lax.axis_size("tm"), lax.axis_size("head")
    tokens, features = queries.shape
    n_local = features // HD
    width = out_weight.shape[1]
    hops = n_head // 2
    dma = pltpu.SemaphoreType.DMA
    hbm_spec = pl.BlockSpec(memory_space=pltpu.HBM)
    projected = pl.pallas_call(
        functools.partial(kernel, n_tm, n_head, n_local),
        out_shape=jax.ShapeDtypeStruct((tokens // n_head, width), jnp.float32),
        in_specs=[hbm_spec] * 4 + [pl.BlockSpec(memory_space=pltpu.SMEM)],
        out_specs=hbm_spec,
        scratch_shapes=[
            pltpu.VMEM((tokens, features), jnp.bfloat16),
            pltpu.VMEM((n_local, tokens, HD), jnp.bfloat16),
            pltpu.VMEM((n_local, TILE, n_head * HD), jnp.bfloat16),
            pltpu.VMEM((n_local, n_head, HD, width), jnp.bfloat16),
            pltpu.VMEM((tokens // n_head, width), jnp.float32),
        ] + [pltpu.VMEM((3 * tokens // TILE, TILE, HD), jnp.bfloat16)] * (2 * n_local) + [
            dma((3 * n_local + 1,)), dma((width // 512,)),
            dma((2 * n_local,)), dma((2 * n_local,)), dma((2 * n_local,)), dma((2 * n_local,)),
            dma((n_local, n_head)), dma((n_local, n_head)),
            dma((n_local, hops, 2, 2)), dma((n_local, hops, 2, 2)),
            dma((n_local, hops, 2, 2)), dma((n_local, hops, 2, 2)),
            dma((n_local, hops, 2)), dma((n_local, hops, 2)),
        ],
        compiler_params=pltpu.CompilerParams(
            collective_id=0, has_side_effects=True, vmem_limit_bytes=VMEM_LIMIT << 20),
        name="attend_and_project",
    )(queries, by_tile(key_rows), by_tile(values), out_weight, window.transpose(2, 0, 1))
    return gate_scale[None, :] * projected


def solution(mesh):
    placed = (
        P(("prompt", "tm"), "head"),
        P(("prompt", "tm"), "head"),
        P(("prompt", "tm"), "head"),
        P("head", None),
        P("prompt"),
        P(("prompt", "tm"), None, None),
    )
    return jax.shard_map(
        body,
        mesh=mesh,
        in_specs=placed,
        out_specs=P(("prompt", "tm", "head"), None),
        check_vma=False,
    )
```
